128 devices in a mesh: dp: 8 (over z, core), tensor: 16 (over y, x).
Axes of the slice: x: 4, y: 4, z: 4, core: 2. Of those that a mesh axis runs over, the one named last changes fastest.
Arguments:
- activations: bfloat16 [65536, 4096], P(('dp', 'tensor')), may hold values from -6 to 6
- cotangent: bfloat16 [65536, 11008], P('dp', 'tensor'), may hold values from -0.008178711 to 0.008178711
- projection: bfloat16 [4096, 512], replicated, may hold values from -0.25 to 0.25
- first_moment: float32 [512, 11008], P('dp', 'tensor'), may hold values from -0.6 to 0.6
- second_moment: float32 [512, 11008], P('dp', 'tensor'), may hold values from 0.01 to 1
- step_count: int32 [1], replicated, may hold values from 1 to 39
Outputs:
- update: bfloat16 [4096, 11008], P('dp', 'tensor')
- new_first: float32 [512, 11008], P('dp', 'tensor')
- new_second: float32 [512, 11008], P('dp', 'tensor')
The draws below stay inside these ranges and needn't reach their ends.
All inputs are finite; a program needn't handle non-finite values.
Results may differ from the reference program's by a relative error of at most 0.0055.
Values may be sent and summed in bfloat16 or wider, within the bound.
A program may use at most 128 MiB of HBM per device.

```python
import math
import jax
import jax.numpy as jnp
from jax import lax

D = 4096
F = 11008
R = 512
TOKENS = 65536


def block_scale(rng, extent, pieces, least, top_value):
    loudness = 1.0
    for axis_at, blocks in pieces:
        heights = jax.random.uniform(jax.random.fold_in(jax.random.fold_in(rng, 6), axis_at), (blocks,), jnp.float32, least / len(pieces), top_value / len(pieces))
        loudness = loudness * jnp.repeat(jnp.exp(heights), extent[axis_at] // blocks).reshape((-1,) + (1,) * (len(extent) - 1 - axis_at))
    return loudness


def normal_values(stream_key, shape, width, reach, cuts=(), dtype=jnp.bfloat16):
    array = width * jax.random.normal(stream_key, shape, jnp.float32)
    if cuts:
        array = array * block_scale(stream_key, shape, cuts, -0.22, 0.18)
    return jnp.clip(array, -reach, reach).astype(dtype)


def setup_inputs(seed: int = 0) -> dict:
    seeds = jax.random.split(jax.random.key(seed), 7)
    return {
        "activations": normal_values(seeds[0], (TOKENS, D), 1.0, 6.0, ((0, 128),)),
        "cotangent": normal_values(seeds[1], (TOKENS, F), (0.35 / (TOKENS) ** 0.5), 0.008178711, ((0, 8), (1, 16))),
        "projection": normal_values(seeds[2], (D, R), R ** -0.5, 0.25),
        "first_moment": normal_values(seeds[3], (R, F), 0.1, 0.6, ((0, 8), (1, 16)), jnp.float32),
        "second_moment": jnp.clip(jnp.exp(math.log(1.0) - 4.6051702 * jax.random.uniform(seeds[4], (R, F), jnp.float32) ** block_scale(seeds[4], (R, F), ((0, 8), (1, 16)), -0.2, 0.2)), 0.01, 1.0),
        "step_count": jax.random.randint(seeds[5], (1,), 1, 40).astype(jnp.int32),
    }


def reference(activations, cotangent, projection, first_moment, second_moment, step_count):
    projected = jnp.dot(activations, projection, preferred_element_type=jnp.float32).astype(jnp.bfloat16)
    grad = lax.dot_general(projected, cotangent, (((0,), (0,)), ((), ())), preferred_element_type=jnp.float32)
    t_value = step_count[0].astype(jnp.float32)
    new_first = 0.9 * first_moment + 0.1 * grad
    new_second = 0.999 * second_moment + 0.001 * grad * grad
    first_hat = new_first / (1.0 - jnp.power(jnp.float32(0.9), t_value))
    second_hat = new_second / (1.0 - jnp.power(jnp.float32(0.999), t_value))
    normalized = (first_hat / (jnp.sqrt(second_hat) + 1e-08)).astype(jnp.bfloat16)
    update = jnp.dot(projection, normalized, preferred_element_type=jnp.float32).astype(jnp.bfloat16)
    return (update, new_first, new_second)
```

```python
import functools

import jax
import jax.numpy as jnp
from jax import lax
from jax.experimental import pallas as pl
from jax.experimental.pallas import tpu as pltpu
from jax.sharding import PartitionSpec as P

MESH = pl.DeviceIdType.MESH
BF, F32 = jnp.bfloat16, jnp.float32
D, F, R = 4096, 11008, 512
TOK = 512
HALF = TOK // 2
NX, NY, NDP = 4, 4, 8
NT = NX * NY
FC = F // NT
DR = D // NDP
PER = R // NDP
CHUNKS = (128, 128, 128, 128)
SHARES = tuple(c // NDP for c in CHUNKS)
STARTS = tuple(sum(SHARES[:i]) for i in range(len(CHUNKS)))
NC = len(CHUNKS)
KSTEPS = 4
KW = D // KSTEPS
GROUP = 4 * HALF
OFFSETS = (0, -1, 1, 2)


def dot(a, b, ca, cb):
    return lax.dot_general(a, b, (((ca,), (cb,)), ((), ())), preferred_element_type=F32)


def identity():
    rows = lax.broadcasted_iota(jnp.int32, (R, R), 0)
    cols = lax.broadcasted_iota(jnp.int32, (R, R), 1)
    return jnp.where(rows == cols, 1.0, 0.0).astype(BF)


def kernel(
    act_hbm, cot_hbm, proj_hbm, first_hbm, second_hbm, step_ref,
    upd_hbm, nfirst_hbm, nsecond_hbm,
    act, proj, cot, first, second, nfirst, nsecond, eye, projt, upd_acc, upd_out,
    *rest,
):
    gath, acc = rest[:NC], rest[NC : 2 * NC]
    part, parts_in = rest[2 * NC : 3 * NC], rest[3 * NC : 4 * NC]
    steps = rest[4 * NC : 5 * NC]
    load_sem, cot_sem, store_sem, ssem, rsem, part_ssem, part_rsem, step_ssem, step_rsem = rest[5 * NC :]

    d = lax.axis_index("dp")
    t = lax.axis_index("tensor")
    y, x = t // NX, t % NX
    pos = ((x, y), (y, x))

    def dev(axis, off):
        if axis == 0:
            return {"dp": d, "tensor": y * NX + (x + off + NX) % NX}
        return {"dp": d, "tensor": ((y + off + NY) % NY) * NX + x}

    def peer(j):
        return {"dp": (d + j) % NDP, "tensor": t}

    loads = []
    for k in range(KSTEPS):
        loads.append(pltpu.make_async_copy(act_hbm.at[:, pl.ds(k * KW, KW)], act.at[:, pl.ds(k * KW, KW)], load_sem.at[2 * k]))
        loads.append(pltpu.make_async_copy(proj_hbm.at[pl.ds(k * KW, KW)], proj.at[pl.ds(k * KW, KW)], load_sem.at[2 * k + 1]))
    loads.append(pltpu.make_async_copy(first_hbm, first, load_sem.at[2 * KSTEPS]))
    loads.append(pltpu.make_async_copy(second_hbm, second, load_sem.at[2 * KSTEPS + 1]))
    for c in loads[: 2 * KSTEPS]:
        c.start()

    barrier = pltpu.get_barrier_semaphore()
    for axis in (0, 1):
        for off in (1, -1):
            pl.semaphore_signal(barrier, inc=1, device_id=dev(axis, off), device_id_type=MESH)
    for j in range(1, NDP):
        pl.semaphore_signal(barrier, inc=1, device_id=peer(j), device_id_type=MESH)

    cot_loads = {}
    for h in (0, 1):
        for v in range(4):
            for u in range(4):
                tt = v * NX + u if h == 0 else u * NX + v
                cot_loads[h, v, u] = pltpu.make_async_copy(
                    cot_hbm.at[:, pl.ds(tt * TOK + h * HALF, HALF)],
                    cot.at[h, v, u],
                    cot_sem.at[h, v, u],
                )
    eye[...] = identity()

    def block(c, h, u, v, q):
        first_pos, second_pos = pos[h]
        ref = gath[c].at[h, (second_pos + v + 4) % 4, (first_pos + u + 4) % 4]
        if q is not None:
            ref = ref.at[pl.ds(q * (CHUNKS[c] // 2), CHUNKS[c] // 2)]
        return ref

    def send(c, h, i, order, off, u, v, q):
        ref = block(c, h, u, v, q)
        pltpu.make_async_remote_copy(
            ref, ref, ssem.at[c, h, i], rsem.at[c, h, i],
            device_id=dev(order ^ h, off), device_id_type=MESH,
        ).start()

    def arrived(c, h, i, u, v, q):
        ref = block(c, h, u, v, q)
        pltpu.make_async_copy(ref, ref, rsem.at[c, h, i]).wait()

    def own_first(c, h):
        send(c, h, 0, 0, 1, 0, 0, None)
        send(c, h, 1, 0, -1, 0, 0, None)

    def to_second(c, h, k):
        send(c, h, 4 + 4 * k, 1, 1, OFFSETS[k], 0, None)
        send(c, h, 5 + 4 * k, 1, -1, OFFSETS[k], 0, None)

    def pass_first(c):
        for h in (0, 1):
            arrived(c, h, 0, -1, 0, None)
            send(c, h, 2, 0, 1, -1, 0, 0)
            arrived(c, h, 1, 1, 0, None)
            send(c, h, 3, 0, -1, 1, 0, 1)
        for h in (0, 1):
            to_second(c, h, 1)
            to_second(c, h, 2)

    def far_first(c):
        for h in (0, 1):
            arrived(c, h, 2, 2, 0, 0)
            arrived(c, h, 3, 2, 0, 1)
            to_second(c, h, 3)

    def pass_second(c, h, k):
        arrived(c, h, 4 + 4 * k, OFFSETS[k], -1, None)
        send(c, h, 6 + 4 * k, 1, 1, OFFSETS[k], -1, 0)
        arrived(c, h, 5 + 4 * k, OFFSETS[k], 1, None)
        send(c, h, 7 + 4 * k, 1, -1, OFFSETS[k], 1, 1)

    def far_second(c, h):
        for k in range(4):
            arrived(c, h, 6 + 4 * k, OFFSETS[k], 2, 0)
            arrived(c, h, 7 + 4 * k, OFFSETS[k], 2, 1)

    def sent(c):
        for h in (0, 1):
            for i in range(20):
                whole = i in (0, 1) or (i >= 4 and i % 4 in (0, 1))
                ref = block(c, h, 0, 0, None if whole else 0)
                pltpu.make_async_copy(ref, ref, ssem.at[c, h, i]).wait()

    def add_group(c, h, v, fresh=False):
        place = (pos[h][1] + v + 4) % 4
        p = jnp.concatenate([gath[c][h, place, u] for u in range(4)], axis=1)
        g = jnp.concatenate([cot[h, place, u] for u in range(4)], axis=1)
        value = dot(p, g, 1, 1)
        if fresh:
            acc[c][...] = value
        else:
            acc[c][...] += value

    def part_copy(c, j):
        return pltpu.make_async_remote_copy(
            part[c].at[(d + j) % NDP], parts_in[c].at[j - 1], part_ssem.at[c, j - 1], part_rsem.at[c, j - 1],
            device_id=peer(j), device_id_type=MESH,
        )

    def step_copy(c, j):
        return pltpu.make_async_remote_copy(
            steps[c].at[d], steps[c].at[d], step_ssem.at[c, j - 1], step_rsem.at[c, j - 1],
            device_id=peer(j), device_id_type=MESH,
        )

    def share_parts(c):
        share = SHARES[c]
        part[c][...] = acc[c][...].reshape(NDP, share, FC).astype(BF)
        for j in range(1, NDP):
            part_copy(c, j).start()

    def adam(c):
        share, start = SHARES[c], STARTS[c]
        t_value = jnp.full((8, 128), step_ref[0].astype(F32), F32)
        fix_first = (1.0 / (1.0 - jnp.power(jnp.full((8, 128), 0.9, F32), t_value)))[0:1, 0:1]
        fix_second = (1.0 / (1.0 - jnp.power(jnp.full((8, 128), 0.999, F32), t_value)))[0:1, 0:1]
        grad = acc[c][pl.ds(pl.multiple_of(d * share, share), share), :]
        for j in range(1, NDP):
            part_copy(c, j).wait_recv()
            grad = grad + parts_in[c][j - 1].astype(F32)
        rows = pl.ds(start, share)
        new_first = 0.9 * first[rows, :] + 0.1 * grad
        new_second = 0.999 * second[rows, :] + 0.001 * grad * grad
        nfirst[rows, :] = new_first
        nsecond[rows, :] = new_second
        normalized = (new_first * fix_first) / (jnp.sqrt(new_second * fix_second) + 1e-08)
        steps[c][d] = normalized.astype(BF)
        for j in range(1, NDP):
            step_copy(c, j).start()

    def update(c):
        for j in range(1, NDP):
            step_copy(c, j).wait_recv()
        chunk = steps[c][...].astype(F32).reshape(CHUNKS[c], FC)
        value = dot(chunk.T.astype(BF), projt[pl.ds(sum(CHUNKS[:c]), CHUNKS[c]), :], 1, 0)
        if c == 0:
            upd_acc[...] = value
        elif c < NC - 1:
            upd_acc[...] += value
        else:
            upd_out[...] = (upd_acc[...] + value).astype(BF)

    for h in (0, 1):
        total = None
        for k in range(KSTEPS):
            if h == 0:
                loads[2 * k].wait()
                loads[2 * k + 1].wait()
            value = dot(act[pl.ds(h * HALF, HALF), pl.ds(k * KW, KW)], proj[pl.ds(k * KW, KW), :], 1, 0)
            total = value if total is None else total + value
        turned = dot(eye[...], total.astype(BF), 1, 1)
        for c in range(NC):
            rows = [turned[PER * e + STARTS[c] : PER * e + STARTS[c] + SHARES[c]] for e in range(NDP)]
            gath[c][h, pos[h][1], pos[h][0]] = jnp.concatenate(rows, axis=0).astype(BF)
        if h == 0:
            pl.semaphore_wait(barrier, 4 + NDP - 1)
            for c in loads[2 * KSTEPS :]:
                c.start()
            for c in cot_loads.values():
                c.start()
        for c in range(NC):
            own_first(c, h)
            if c < 2:
                to_second(c, h, 0)
    turned = dot(eye[...], proj[pl.ds(pl.multiple_of(d * DR, DR), DR), :], 1, 1)
    for c in range(NC):
        rows = [turned[PER * e + STARTS[c] : PER * e + STARTS[c] + SHARES[c]] for e in range(NDP)]
        projt[pl.ds(sum(CHUNKS[:c]), CHUNKS[c]), :] = jnp.concatenate(rows, axis=0).astype(BF)

    for i in range(NC + 2):
        if i < NC:
            pass_first(i)
            far_first(i)
            if 2 <= i + 1 < NC:
                for h in (0, 1):
                    to_second(i + 1, h, 0)
            if i == 0:
                for c in loads[2 * KSTEPS :]:
                    c.wait()
                for c in cot_loads.values():
                    c.wait()
        c = i - 1
        if 0 <= c < NC:
            for h in (0, 1):
                for k in range(4):
                    pass_second(c, h, k)
        if i < NC:
            add_group(i, 0, 0, fresh=True)
            add_group(i, 1, 0)
        if 0 <= c < NC:
            for h in (0, 1):
                add_group(c, h, -1)
                add_group(c, h, 1)
        c = i - 2
        if 0 <= c < NC:
            for h in (0, 1):
                far_second(c, h)
                add_group(c, h, 2)
            share_parts(c)
        if 0 <= c - 1:
            adam(c - 1)
        if 0 <= c - 2:
            update(c - 2)
    for c in range(NC):
        sent(c)
    update(NC - 2)
    for c in range(NC - 1):
        for j in range(1, NDP):
            part_copy(c, j).wait_send()
            step_copy(c, j).wait_send()
    adam(NC - 1)
    stores = [
        pltpu.make_async_copy(nfirst, nfirst_hbm, store_sem.at[0]),
        pltpu.make_async_copy(nsecond, nsecond_hbm, store_sem.at[1]),
        pltpu.make_async_copy(upd_out, upd_hbm, store_sem.at[2]),
    ]
    stores[0].start()
    stores[1].start()
    update(NC - 1)
    stores[2].start()
    for j in range(1, NDP):
        part_copy(NC - 1, j).wait_send()
        step_copy(NC - 1, j).wait_send()
    for c in stores:
        c.wait()


def per_device(activations, cotangent, projection, first_moment, second_moment, step_count):
    anywhere = pl.BlockSpec(memory_space=pl.ANY)
    scratch = [
        pltpu.VMEM((TOK, D), BF),
        pltpu.VMEM((D, R), BF),
        pltpu.VMEM((2, 4, 4, FC, HALF), BF),
        pltpu.VMEM((PER, FC), F32),
        pltpu.VMEM((PER, FC), F32),
        pltpu.VMEM((PER, FC), F32),
        pltpu.VMEM((PER, FC), F32),
        pltpu.VMEM((R, R), BF),
        pltpu.VMEM((R, DR), BF),
        pltpu.VMEM((FC, DR), F32),
        pltpu.VMEM((FC, DR), BF),
    ]
    scratch += [pltpu.VMEM((2, 4, 4, c, HALF), BF) for c in CHUNKS]
    scratch += [pltpu.VMEM((c, FC), F32) for c in CHUNKS]
    scratch += [pltpu.VMEM((NDP, s, FC), BF) for s in SHARES]
    scratch += [pltpu.VMEM((NDP - 1, s, FC), BF) for s in SHARES]
    scratch += [pltpu.VMEM((NDP, s, FC), BF) for s in SHARES]
    dma = pltpu.SemaphoreType.DMA
    scratch += [
        dma((2 * KSTEPS + 2,)), dma((2, 4, 4)), dma((3,)), dma((NC, 2, 20)), dma((NC, 2, 20)),
        dma((NC, NDP - 1)), dma((NC, NDP - 1)), dma((NC, NDP - 1)), dma((NC, NDP - 1)),
    ]
    update_t, new_first, new_second = pl.pallas_call(
        kernel,
        out_shape=(
            jax.ShapeDtypeStruct((FC, DR), BF),
            jax.ShapeDtypeStruct((PER, FC), F32),
            jax.ShapeDtypeStruct((PER, FC), F32),
        ),
        in_specs=[anywhere] * 5 + [pl.BlockSpec(memory_space=pltpu.SMEM)],
        out_specs=[anywhere] * 3,
        scratch_shapes=scratch,
        compiler_params=pltpu.CompilerParams(
            collective_id=0, has_side_effects=True, vmem_limit_bytes=56 * 2**20
        ),
        cost_estimate=pl.CostEstimate(flops=9 * 10**9, bytes_accessed=25 * 10**6, transcendentals=0),
    )(activations, cotangent.T, projection, first_moment, second_moment, step_count)
    return update_t.T, new_first, new_second


def solution(mesh):
    in_specs = (
        P(("dp", "tensor"), None),
        P("dp", "tensor"),
        P(),
        P("dp", "tensor"),
        P("dp", "tensor"),
        P(),
    )
    out_specs = (P("dp", "tensor"), P("dp", "tensor"), P("dp", "tensor"))
    return jax.shard_map(
        per_device, mesh=mesh, in_specs=in_specs, out_specs=out_specs, check_vma=False
    )
```

```python
import functools

import jax
import jax.numpy as jnp
from jax import lax
from jax.experimental import pallas as pl
from jax.experimental.pallas import tpu as pltpu
from jax.sharding import PartitionSpec as P

MESH = pl.DeviceIdType.MESH
BF, F32 = jnp.bfloat16, jnp.float32
D, F, R = 4096, 11008, 512
TOK = 512
HALF = TOK // 2
NX, NY, NDP = 4, 4, 8
NT = NX * NY
FC = F // NT
DR = D // NDP
PER = R // NDP
CHUNKS = (128, 128, 128, 128)
SHARES = tuple(c // NDP for c in CHUNKS)
STARTS = tuple(sum(SHARES[:i]) for i in range(len(CHUNKS)))
NC = len(CHUNKS)
KSTEPS = 4
KW = D // KSTEPS
GROUP = 4 * HALF
VMEM_MIB = 52
OFFSETS = (0, -1, 1, 2)


def dot(a, b, ca, cb):
    return lax.dot_general(a, b, (((ca,), (cb,)), ((), ())), preferred_element_type=F32)


def identity():
    rows = lax.broadcasted_iota(jnp.int32, (R, R), 0)
    cols = lax.broadcasted_iota(jnp.int32, (R, R), 1)
    return jnp.where(rows == cols, 1.0, 0.0).astype(BF)


def kernel(
    act_hbm, cot_hbm, proj_hbm, first_hbm, second_hbm, step_hbm,
    upd_out, nfirst, nsecond,
    step_now, act, proj, cot, first, second, eye, projt, upd_acc,
    *rest,
):
    gath, acc = rest[:NC], rest[NC : 2 * NC]
    part, parts_in = rest[2 * NC : 3 * NC], rest[3 * NC : 4 * NC]
    steps = rest[4 * NC : 5 * NC]
    load_sem, cot_sem, ssem, rsem, part_ssem, part_rsem, step_ssem, step_rsem = rest[5 * NC :]

    d = lax.axis_index("dp")
    t = lax.axis_index("tensor")
    y, x = t // NX, t % NX
    pos = ((x, y), (y, x))

    def dev(axis, off):
        if axis == 0:
            return {"dp": d, "tensor": y * NX + (x + off + NX) % NX}
        return {"dp": d, "tensor": ((y + off + NY) % NY) * NX + x}

    def peer(j):
        return {"dp": (d + j) % NDP, "tensor": t}

    loads = []
    for k in range(KSTEPS):
        loads.append(pltpu.make_async_copy(act_hbm.at[:, pl.ds(k * KW, KW)], act.at[:, pl.ds(k * KW, KW)], load_sem.at[2 * k]))
        loads.append(pltpu.make_async_copy(proj_hbm.at[pl.ds(k * KW, KW)], proj.at[pl.ds(k * KW, KW)], load_sem.at[2 * k + 1]))
    loads.append(pltpu.make_async_copy(first_hbm, first, load_sem.at[2 * KSTEPS]))
    loads.append(pltpu.make_async_copy(second_hbm, second, load_sem.at[2 * KSTEPS + 1]))
    loads.append(pltpu.make_async_copy(step_hbm, step_now, load_sem.at[2 * KSTEPS + 2]))
    for c in loads[: 2 * KSTEPS]:
        c.start()

    barrier = pltpu.get_barrier_semaphore()
    for axis in (0, 1):
        for off in (1, -1):
            pl.semaphore_signal(barrier, inc=1, device_id=dev(axis, off), device_id_type=MESH)
    for j in range(1, NDP):
        pl.semaphore_signal(barrier, inc=1, device_id=peer(j), device_id_type=MESH)

    cot_loads = {}
    for h in (0, 1):
        for v in range(4):
            for u in range(4):
                tt = v * NX + u if h == 0 else u * NX + v
                cot_loads[h, v, u] = pltpu.make_async_copy(
                    cot_hbm.at[:, pl.ds(tt * TOK + h * HALF, HALF)],
                    cot.at[h, v * 4 + u],
                    cot_sem.at[0],
                )
    eye[...] = identity()

    def place(h, u, v):
        first_pos, second_pos = pos[h]
        return ((second_pos + v + 4) % 4) * 4 + (first_pos + u + 4) % 4

    def send(c, h, i, order, off, u, v, q):
        ref = gath[c].at[h, place(h, u, v)]
        if q is not None:
            ref = ref.at[pl.ds(q * (CHUNKS[c] // 2), CHUNKS[c] // 2)]
        pltpu.make_async_remote_copy(
            ref, ref, ssem.at[c, h], rsem.at[c, h, i],
            device_id=dev(order ^ h, off), device_id_type=MESH,
        ).start()

    def arrived(c, h, i, blocks):
        ref = gath[c].at[h, pl.ds(0, blocks)]
        pltpu.make_async_copy(ref, ref, rsem.at[c, h, i]).wait()

    def own_first(c, h):
        send(c, h, 0, 0, 1, 0, 0, None)
        send(c, h, 0, 0, -1, 0, 0, None)

    def to_second(c, h, k):
        send(c, h, 2 + k, 1, 1, OFFSETS[k], 0, None)
        send(c, h, 2 + k, 1, -1, OFFSETS[k], 0, None)

    def pass_first(c):
        for h in (0, 1):
            arrived(c, h, 0, 2)
            send(c, h, 1, 0, 1, -1, 0, 0)
            send(c, h, 1, 0, -1, 1, 0, 1)

    def far_first(c):
        for h in (0, 1):
            arrived(c, h, 1, 1)

    def pass_second(c, h, k):
        arrived(c, h, 2 + k, 2)
        send(c, h, 6, 1, 1, OFFSETS[k], -1, 0)
        send(c, h, 6, 1, -1, OFFSETS[k], 1, 1)

    def far_second(c, h):
        arrived(c, h, 6, 4)

    def sent(c):
        for h in (0, 1):
            ref = gath[c].at[h, pl.ds(0, 15)]
            pltpu.make_async_copy(ref, ref, ssem.at[c, h]).wait()

    def add_group(c, h, v, fresh=False):
        at = ((pos[h][1] + v + 4) % 4) * 4
        p = jnp.concatenate([gath[c][h, at + u] for u in range(4)], axis=1)
        g = jnp.concatenate([cot[h, at + u] for u in range(4)], axis=1)
        value = dot(p, g, 1, 1)
        if fresh:
            acc[c][...] = value
        else:
            acc[c][...] += value

    def part_copy(c, j):
        return pltpu.make_async_remote_copy(
            part[c].at[(d + j) % NDP], parts_in[c].at[j - 1], part_ssem.at[c], part_rsem.at[c],
            device_id=peer(j), device_id_type=MESH,
        )

    def step_copy(c, j):
        return pltpu.make_async_remote_copy(
            steps[c].at[d], steps[c].at[d], step_ssem.at[c], step_rsem.at[c],
            device_id=peer(j), device_id_type=MESH,
        )

    def share_parts(c):
        share = SHARES[c]
        part[c][...] = acc[c][...].reshape(NDP, share, FC).astype(BF)
        for j in range(1, NDP):
            part_copy(c, j).start()

    def adam(c):
        share, start = SHARES[c], STARTS[c]
        t_value = jnp.full((8, 128), step_now[0].astype(F32), F32)
        fix_first = (1.0 / (1.0 - jnp.power(jnp.full((8, 128), 0.9, F32), t_value)))[0:1, 0:1]
        fix_second = (1.0 / (1.0 - jnp.power(jnp.full((8, 128), 0.999, F32), t_value)))[0:1, 0:1]
        grad = acc[c][pl.ds(pl.multiple_of(d * share, share), share), :]
        pltpu.make_async_copy(parts_in[c], parts_in[c], part_rsem.at[c]).wait()
        for j in range(1, NDP):
            grad = grad + parts_in[c][j - 1].astype(F32)
        rows = pl.ds(start, share)
        new_first = 0.9 * first[rows, :] + 0.1 * grad
        new_second = 0.999 * second[rows, :] + 0.001 * grad * grad
        nfirst[rows, :] = new_first
        nsecond[rows, :] = new_second
        normalized = (new_first * fix_first) / (jnp.sqrt(new_second * fix_second) + 1e-08)
        steps[c][d] = normalized.astype(BF)
        for j in range(1, NDP):
            step_copy(c, j).start()

    def update(c):
        seven = steps[c].at[pl.ds(0, NDP - 1)]
        pltpu.make_async_copy(seven, seven, step_rsem.at[c]).wait()
        chunk = steps[c][...].astype(F32).reshape(CHUNKS[c], FC)
        value = dot(chunk.T.astype(BF), projt[pl.ds(sum(CHUNKS[:c]), CHUNKS[c]), :], 1, 0)
        if c == 0:
            upd_acc[...] = value
        elif c < NC - 1:
            upd_acc[...] += value
        else:
            upd_out[...] = (upd_acc[...] + value).astype(BF)

    for h in (0, 1):
        total = None
        for k in range(KSTEPS):
            if h == 0:
                loads[2 * k].wait()
                loads[2 * k + 1].wait()
            value = dot(act[pl.ds(h * HALF, HALF), pl.ds(k * KW, KW)], proj[pl.ds(k * KW, KW), :], 1, 0)
            total = value if total is None else total + value
        turned = dot(eye[...], total.astype(BF), 1, 1)
        for c in range(NC):
            rows = [turned[PER * e + STARTS[c] : PER * e + STARTS[c] + SHARES[c]] for e in range(NDP)]
            gath[c][h, place(h, 0, 0)] = jnp.concatenate(rows, axis=0).astype(BF)
        if h == 0:
            pl.semaphore_wait(barrier, 4 + NDP - 1)
            for c in loads[2 * KSTEPS :]:
                c.start()
            for c in cot_loads.values():
                c.start()
        own_first(0, h)
        to_second(0, h, 0)
    for c in range(1, NC):
        for h in (0, 1):
            own_first(c, h)
    turned = dot(eye[...], proj[pl.ds(pl.multiple_of(d * DR, DR), DR), :], 1, 1)
    for c in range(NC):
        rows = [turned[PER * e + STARTS[c] : PER * e + STARTS[c] + SHARES[c]] for e in range(NDP)]
        projt[pl.ds(sum(CHUNKS[:c]), CHUNKS[c]), :] = jnp.concatenate(rows, axis=0).astype(BF)

    pass_first(0)
    for k in (1, 2):
        for h in (0, 1):
            to_second(0, h, k)
    for c in range(1, NC):
        pass_first(c)
    far_first(0)
    for h in (0, 1):
        to_second(0, h, 3)
    for c in range(1, NC):
        far_first(c)
    for c in loads[2 * KSTEPS :]:
        c.wait()
    pltpu.make_async_copy(cot, cot, cot_sem.at[0]).wait()

    for i in range(NC):
        if i + 1 < NC:
            for k in range(4):
                for h in (0, 1):
                    to_second(i + 1, h, k)
        for k in range(4):
            for h in (0, 1):
                pass_second(i, h, k)
            if k == 0:
                add_group(i, 0, 0, fresh=True)
            if k == 1:
                add_group(i, 1, 0)
                if i >= 2:
                    adam(i - 2)
            if k == 2 and i >= 3:
                update(i - 3)
        add_group(i, 0, -1)
        add_group(i, 0, 1)
        if i >= 1:
            for h in (0, 1):
                far_second(i - 1, h)
                add_group(i - 1, h, 2)
            share_parts(i - 1)
        add_group(i, 1, -1)
        add_group(i, 1, 1)
    for h in (0, 1):
        far_second(NC - 1, h)
        add_group(NC - 1, h, 2)
    share_parts(NC - 1)
    adam(NC - 2)
    update(NC - 3)
    for c in range(NC):
        sent(c)
    for c in range(NC - 1):
        pltpu.make_async_copy(parts_in[c], parts_in[c], part_ssem.at[c]).wait()
    adam(NC - 1)
    for c in range(NC - 1):
        seven = steps[c].at[pl.ds(0, NDP - 1)]
        pltpu.make_async_copy(seven, seven, step_ssem.at[c]).wait()
    update(NC - 2)
    update(NC - 1)
    pltpu.make_async_copy(parts_in[NC - 1], parts_in[NC - 1], part_ssem.at[NC - 1]).wait()
    seven = steps[NC - 1].at[pl.ds(0, NDP - 1)]
    pltpu.make_async_copy(seven, seven, step_ssem.at[NC - 1]).wait()


def write_out(*arrays):
    def body(*refs):
        n = len(arrays)
        copies = [
            pltpu.make_async_copy(refs[i], refs[n + i], refs[2 * n].at[i]) for i in range(n)
        ]
        for c in copies:
            c.start()
        for c in copies:
            c.wait()

    return pl.pallas_call(
        body,
        out_shape=tuple(jax.ShapeDtypeStruct(a.shape, a.dtype) for a in arrays),
        in_specs=[pl.BlockSpec(memory_space=pltpu.VMEM)] * len(arrays),
        out_specs=[pl.BlockSpec(memory_space=pltpu.HBM)] * len(arrays),
        scratch_shapes=[pltpu.SemaphoreType.DMA((len(arrays),))],
        compiler_params=pltpu.CompilerParams(vmem_limit_bytes=2 * 2**20),
    )(*arrays)


def per_device(activations, cotangent, projection, first_moment, second_moment, step_count):
    scratch = [
        pltpu.SMEM((1,), jnp.int32),
        pltpu.VMEM((TOK, D), BF),
        pltpu.VMEM((D, R), BF),
        pltpu.VMEM((2, NT, FC, HALF), BF),
        pltpu.VMEM((PER, FC), F32),
        pltpu.VMEM((PER, FC), F32),
        pltpu.VMEM((R, R), BF),
        pltpu.VMEM((R, DR), BF),
        pltpu.VMEM((FC, DR), F32),
    ]
    scratch += [pltpu.VMEM((2, NT, c, HALF), BF) for c in CHUNKS]
    scratch += [pltpu.VMEM((c, FC), F32) for c in CHUNKS]
    scratch += [pltpu.VMEM((NDP, s, FC), BF) for s in SHARES]
    scratch += [pltpu.VMEM((NDP - 1, s, FC), BF) for s in SHARES]
    scratch += [pltpu.VMEM((NDP, s, FC), BF) for s in SHARES]
    dma = pltpu.SemaphoreType.DMA
    scratch += [
        dma((2 * KSTEPS + 3,)), dma((1,)), dma((NC, 2)), dma((NC, 2, 7)),
        dma((NC,)), dma((NC,)), dma((NC,)), dma((NC,)),
    ]
    update_t, new_first, new_second = pl.pallas_call(
        kernel,
        out_shape=(
            jax.ShapeDtypeStruct((FC, DR), BF),
            jax.ShapeDtypeStruct((PER, FC), F32),
            jax.ShapeDtypeStruct((PER, FC), F32),
        ),
        in_specs=[pl.BlockSpec(memory_space=pltpu.HBM)] * 6,
        out_specs=[pl.BlockSpec(memory_space=pltpu.VMEM)] * 3,
        scratch_shapes=scratch,
        compiler_params=pltpu.CompilerParams(
            collective_id=0, has_side_effects=True, vmem_limit_bytes=int(VMEM_MIB * 2**20)
        ),
        cost_estimate=pl.CostEstimate(flops=9 * 10**9, bytes_accessed=25 * 10**6, transcendentals=0),
    )(activations, cotangent.T, projection, first_moment, second_moment, step_count)
    update_t, new_first, new_second = write_out(update_t, new_first, new_second)
    return update_t.T, new_first, new_second


def solution(mesh):
    in_specs = (
        P(("dp", "tensor"), None),
        P("dp", "tensor"),
        P(),
        P("dp", "tensor"),
        P("dp", "tensor"),
        P(),
    )
    out_specs = (P("dp", "tensor"), P("dp", "tensor"), P("dp", "tensor"))
    return jax.shard_map(
        per_device, mesh=mesh, in_specs=in_specs, out_specs=out_specs, check_vma=False
    )
```

```python
import functools

import jax
import jax.numpy as jnp
from jax import lax
from jax.experimental import pallas as pl
from jax.experimental.pallas import tpu as pltpu
from jax.sharding import PartitionSpec as P

MESH = pl.DeviceIdType.MESH
BF, F32 = jnp.bfloat16, jnp.float32
D, F, R = 4096, 11008, 512
TOK = 512
HALF = TOK // 2
NX, NY, NDP = 4, 4, 8
NT = NX * NY
FC = F // NT
DR = D // NDP
PER = R // NDP
CHUNKS = (128, 128, 128, 128)
SHARES = tuple(c // NDP for c in CHUNKS)
STARTS = tuple(sum(SHARES[:i]) for i in range(len(CHUNKS)))
NC = len(CHUNKS)
PIECES = tuple((c, 0, FC) for c in range(NC - 1)) + ((NC - 1, 0, 384), (NC - 1, 384, FC - 384))
NP = len(PIECES)
PIECES_OF = tuple(tuple(p for p in range(NP) if PIECES[p][0] == c) for c in range(NC))
PART_TYPES = tuple(BF for c, _, _ in PIECES)
KSTEPS = 4
KW = D // KSTEPS
GROUP = 4 * HALF
VMEM_MIB = 52
OFFSETS = (0, -1, 1, 2)


def dot(a, b, ca, cb):
    return lax.dot_general(a, b, (((ca,), (cb,)), ((), ())), preferred_element_type=F32)


def identity():
    rows = lax.broadcasted_iota(jnp.int32, (R, R), 0)
    cols = lax.broadcasted_iota(jnp.int32, (R, R), 1)
    return jnp.where(rows == cols, 1.0, 0.0).astype(BF)


def kernel(
    act_hbm, cot_hbm, proj_hbm, step_hbm, state,
    upd_out, nfirst, nsecond,
    step_now, act, proj, cot, eye, projt, upd_acc,
    *rest,
):
    gath, acc = rest[:NC], rest[NC : 2 * NC]
    rest = rest[2 * NC :]
    part, parts_in, steps = rest[:NP], rest[NP : 2 * NP], rest[2 * NP : 3 * NP]
    load_sem, cot_sem, ssem, rsem, part_ssem, part_rsem, step_ssem, step_rsem = rest[3 * NP :]

    d = lax.axis_index("dp")
    t = lax.axis_index("tensor")
    y, x = t // NX, t % NX
    pos = ((x, y), (y, x))

    def dev(axis, off):
        if axis == 0:
            return {"dp": d, "tensor": y * NX + (x + off + NX) % NX}
        return {"dp": d, "tensor": ((y + off + NY) % NY) * NX + x}

    def peer(j):
        return {"dp": (d + j) % NDP, "tensor": t}

    loads = []
    for k in range(KSTEPS):
        part_k = (pl.ds(0, HALF), pl.ds(k * KW, KW))
        loads.append(pltpu.make_async_copy(act_hbm.at[part_k], act.at[part_k], load_sem.at[2 * k]))
        loads.append(pltpu.make_async_copy(proj_hbm.at[pl.ds(k * KW, KW)], proj.at[pl.ds(k * KW, KW)], load_sem.at[2 * k + 1]))
    late = pl.ds(HALF, HALF)
    late_load = pltpu.make_async_copy(act_hbm.at[late], act.at[late], load_sem.at[2 * KSTEPS + 3])
    loads.append(pltpu.make_async_copy(step_hbm, step_now, load_sem.at[2 * KSTEPS + 2]))
    for c in loads[: 2 * KSTEPS]:
        c.start()
    late_load.start()

    barrier = pltpu.get_barrier_semaphore()
    for axis in (0, 1):
        for off in (1, -1):
            pl.semaphore_signal(barrier, inc=1, device_id=dev(axis, off), device_id_type=MESH)
    for j in range(1, NDP):
        pl.semaphore_signal(barrier, inc=1, device_id=peer(j), device_id_type=MESH)

    cot_loads = {}
    for h in (0, 1):
        for v in range(4):
            for u in range(4):
                tt = v * NX + u if h == 0 else u * NX + v
                cot_loads[h, v, u] = pltpu.make_async_copy(
                    cot_hbm.at[:, pl.ds(tt * TOK + h * HALF, HALF)],
                    cot.at[h, v * 4 + u],
                    cot_sem.at[0],
                )
    eye[...] = identity()

    def place(h, u, v):
        first_pos, second_pos = pos[h]
        return ((second_pos + v + 4) % 4) * 4 + (first_pos + u + 4) % 4

    def send(c, h, i, order, off, u, v, q):
        ref = gath[c].at[h, place(h, u, v)]
        if q is not None:
            ref = ref.at[pl.ds(q * (CHUNKS[c] // 2), CHUNKS[c] // 2)]
        pltpu.make_async_remote_copy(
            ref, ref, ssem.at[c, h], rsem.at[c, h, i],
            device_id=dev(order ^ h, off), device_id_type=MESH,
        ).start()

    def arrived(c, h, i, blocks):
        ref = gath[c].at[h, pl.ds(0, blocks)]
        pltpu.make_async_copy(ref, ref, rsem.at[c, h, i]).wait()

    def own_first(c, h):
        send(c, h, 0, 0, 1, 0, 0, None)
        send(c, h, 0, 0, -1, 0, 0, None)

    def to_second(c, h, k):
        send(c, h, 2 + k, 1, 1, OFFSETS[k], 0, None)
        send(c, h, 2 + k, 1, -1, OFFSETS[k], 0, None)

    def pass_first(c):
        for h in (0, 1):
            arrived(c, h, 0, 2)
            send(c, h, 1, 0, 1, -1, 0, 0)
            send(c, h, 1, 0, -1, 1, 0, 1)

    def far_first(c):
        for h in (0, 1):
            arrived(c, h, 1, 1)

    def pass_second(c, h, k):
        arrived(c, h, 2 + k, 2)
        send(c, h, 6, 1, 1, OFFSETS[k], -1, 0)
        send(c, h, 6, 1, -1, OFFSETS[k], 1, 1)

    def far_second(c, h):
        arrived(c, h, 6, 4)

    def sent(c):
        for h in (0, 1):
            ref = gath[c].at[h, pl.ds(0, 15)]
            pltpu.make_async_copy(ref, ref, ssem.at[c, h]).wait()

    def add_group(c, h, v, fresh=False):
        at = ((pos[h][1] + v + 4) % 4) * 4
        p = jnp.concatenate([gath[c][h, at + u] for u in range(4)], axis=1)
        g = jnp.concatenate([cot[h, at + u] for u in range(4)], axis=1)
        value = dot(p, g, 1, 1)
        if fresh:
            acc[c][...] = value
        else:
            acc[c][...] += value

    def part_copy(p, j):
        return pltpu.make_async_remote_copy(
            part[p].at[(d + j) % NDP], parts_in[p].at[j - 1], part_ssem.at[p], part_rsem.at[p],
            device_id=peer(j), device_id_type=MESH,
        )

    def step_copy(p, j):
        return pltpu.make_async_remote_copy(
            steps[p].at[d], steps[p].at[d], step_ssem.at[p], step_rsem.at[p],
            device_id=peer(j), device_id_type=MESH,
        )

    def seven(ref, sem):
        ref = ref.at[pl.ds(0, NDP - 1)]
        pltpu.make_async_copy(ref, ref, sem).wait()

    def share_parts(p):
        c, start, width = PIECES[p]
        own = acc[c][:, start : start + width]
        part[p][...] = own.reshape(NDP, SHARES[c], width).astype(PART_TYPES[p])
        for j in range(1, NDP):
            part_copy(p, j).start()

    def adam(p):
        c, start, width = PIECES[p]
        share = SHARES[c]
        cols = slice(start, start + width)
        t_value = step_now[...].astype(F32)
        fix_first = (1.0 / (1.0 - jnp.power(jnp.full((8, 128), 0.9, F32), t_value)))[0:1, 0:1]
        fix_second = (1.0 / (1.0 - jnp.power(jnp.full((8, 128), 0.999, F32), t_value)))[0:1, 0:1]
        grad = acc[c][pl.ds(pl.multiple_of(d * share, share), share), cols]
        seven(parts_in[p], part_rsem.at[p])
        for j in range(1, NDP):
            grad = grad + parts_in[p][j - 1].astype(F32)
        rows = slice(STARTS[c], STARTS[c] + share)
        new_first = 0.9 * state[rows, cols] + 0.1 * grad
        new_second = 0.999 * state[PER + STARTS[c] : PER + STARTS[c] + share, cols] + 0.001 * grad * grad
        nfirst[rows, cols] = new_first
        nsecond[rows, cols] = new_second
        normalized = (new_first * fix_first) / (jnp.sqrt(new_second * fix_second) + 1e-08)
        steps[p][d] = normalized.astype(BF)
        for j in range(1, NDP):
            step_copy(p, j).start()

    def update(p):
        c, start, width = PIECES[p]
        seven(steps[p], step_rsem.at[p])
        chunk = steps[p][...].astype(F32).reshape(CHUNKS[c], width)
        value = dot(chunk.T.astype(BF), projt[pl.ds(sum(CHUNKS[:c]), CHUNKS[c]), :], 1, 0)
        if c == 0:
            upd_acc[...] = value
        elif c < NC - 1:
            upd_acc[...] += value
        else:
            rows = slice(start, start + width)
            upd_out[rows, :] = (upd_acc[rows, :] + value).astype(BF)

    for h in (0, 1):
        total = None
        if h == 1:
            late_load.wait()
        for k in range(KSTEPS):
            if h == 0:
                loads[2 * k].wait()
                loads[2 * k + 1].wait()
            value = dot(act[pl.ds(h * HALF, HALF), pl.ds(k * KW, KW)], proj[pl.ds(k * KW, KW), :], 1, 0)
            total = value if total is None else total + value
        turned = dot(eye[...], total.astype(BF), 1, 1)
        for c in range(NC):
            rows = [turned[PER * e + STARTS[c] : PER * e + STARTS[c] + SHARES[c]] for e in range(NDP)]
            gath[c][h, place(h, 0, 0)] = jnp.concatenate(rows, axis=0).astype(BF)
        if h == 0:
            pl.semaphore_wait(barrier, 4 + NDP - 1)
            for c in loads[2 * KSTEPS :]:
                c.start()
            for c in cot_loads.values():
                c.start()
        own_first(0, h)
        to_second(0, h, 0)
    for c in range(1, NC):
        for h in (0, 1):
            own_first(c, h)
    turned = dot(eye[...], proj[pl.ds(pl.multiple_of(d * DR, DR), DR), :], 1, 1)
    for c in range(NC):
        rows = [turned[PER * e + STARTS[c] : PER * e + STARTS[c] + SHARES[c]] for e in range(NDP)]
        projt[pl.ds(sum(CHUNKS[:c]), CHUNKS[c]), :] = jnp.concatenate(rows, axis=0).astype(BF)

    pass_first(0)
    for k in (1, 2):
        for h in (0, 1):
            to_second(0, h, k)
    for c in range(1, NC):
        pass_first(c)
    far_first(0)
    for h in (0, 1):
        to_second(0, h, 3)
    for c in range(1, NC):
        far_first(c)
    for c in loads[2 * KSTEPS :]:
        c.wait()
    pltpu.make_async_copy(cot, cot, cot_sem.at[0]).wait()

    for i in range(NC):
        if i + 1 < NC:
            for k in range(4):
                for h in (0, 1):
                    to_second(i + 1, h, k)
        for k in range(4):
            for h in (0, 1):
                pass_second(i, h, k)
            if k == 0:
                add_group(i, 0, 0, fresh=True)
            if k == 1:
                add_group(i, 1, 0)
                if i >= 2:
                    adam(i - 2)
            if k == 2 and i >= 3:
                update(i - 3)
        add_group(i, 0, -1)
        add_group(i, 0, 1)
        if i >= 1:
            for h in (0, 1):
                far_second(i - 1, h)
                add_group(i - 1, h, 2)
            share_parts(i - 1)
        add_group(i, 1, -1)
        add_group(i, 1, 1)
    for h in (0, 1):
        far_second(NC - 1, h)
        add_group(NC - 1, h, 2)
    for p in PIECES_OF[NC - 1]:
        share_parts(p)
    adam(NC - 2)
    update(NC - 3)
    for c in range(NC):
        sent(c)
    for p in range(NC - 1):
        seven(parts_in[p], part_ssem.at[p])
    for p in PIECES_OF[NC - 1]:
        adam(p)
    for p in range(NC - 2):
        seven(steps[p], step_ssem.at[p])
    update(NC - 2)
    for p in PIECES_OF[NC - 1]:
        update(p)
    for p in PIECES_OF[NC - 1]:
        seven(parts_in[p], part_ssem.at[p])
    for p in range(NC - 2, NP):
        seven(steps[p], step_ssem.at[p])


def write_out(*arrays):
    def body(*refs):
        n = len(arrays)
        copies = [
            pltpu.make_async_copy(refs[i], refs[n + i], refs[2 * n].at[i]) for i in range(n)
        ]
        for c in copies:
            c.start()
        for c in copies:
            c.wait()

    return pl.pallas_call(
        body,
        out_shape=tuple(jax.ShapeDtypeStruct(a.shape, a.dtype) for a in arrays),
        in_specs=[pl.BlockSpec(memory_space=pltpu.VMEM)] * len(arrays),
        out_specs=[pl.BlockSpec(memory_space=pltpu.HBM)] * len(arrays),
        scratch_shapes=[pltpu.SemaphoreType.DMA((len(arrays),))],
        compiler_params=pltpu.CompilerParams(vmem_limit_bytes=2 * 2**20),
    )(*arrays)


def per_device(activations, cotangent, projection, first_moment, second_moment, step_count):
    scratch = [
        pltpu.VMEM((8, 128), jnp.int32),
        pltpu.VMEM((TOK, D), BF),
        pltpu.VMEM((D, R), BF),
        pltpu.VMEM((2, NT, FC, HALF), BF),
        pltpu.VMEM((R, R), BF),
        pltpu.VMEM((R, DR), BF),
        pltpu.VMEM((FC, DR), F32),
    ]
    scratch += [pltpu.VMEM((2, NT, c, HALF), BF) for c in CHUNKS]
    scratch += [pltpu.VMEM((c, FC), F32) for c in CHUNKS]
    scratch += [pltpu.VMEM((NDP, SHARES[c], w), ty) for (c, _, w), ty in zip(PIECES, PART_TYPES)]
    scratch += [pltpu.VMEM((NDP - 1, SHARES[c], w), ty) for (c, _, w), ty in zip(PIECES, PART_TYPES)]
    scratch += [pltpu.VMEM((NDP, SHARES[c], w), BF) for c, _, w in PIECES]
    dma = pltpu.SemaphoreType.DMA
    scratch += [
        dma((2 * KSTEPS + 4,)), dma((1,)), dma((NC, 2)), dma((NC, 2, 7)),
        dma((NP,)), dma((NP,)), dma((NP,)), dma((NP,)),
    ]
    update_t, new_first, new_second = pl.pallas_call(
        kernel,
        out_shape=(
            jax.ShapeDtypeStruct((FC, DR), BF),
            jax.ShapeDtypeStruct((PER, FC), F32),
            jax.ShapeDtypeStruct((PER, FC), F32),
        ),
        in_specs=[pl.BlockSpec(memory_space=pltpu.HBM)] * 4 + [pl.BlockSpec(memory_space=pltpu.VMEM)],
        out_specs=[pl.BlockSpec(memory_space=pltpu.VMEM)] * 3,
        scratch_shapes=scratch,
        compiler_params=pltpu.CompilerParams(
            collective_id=0, has_side_effects=True, vmem_limit_bytes=int(VMEM_MIB * 2**20)
        ),
        cost_estimate=pl.CostEstimate(flops=9 * 10**9, bytes_accessed=25 * 10**6, transcendentals=0),
    )(activations, cotangent.T, projection, jnp.pad(step_count.reshape(1, 1), ((0, 7), (0, 127))), jnp.concatenate([first_moment, second_moment], axis=0))
    update_t, new_first, new_second = write_out(update_t, new_first, new_second)
    return update_t.T, new_first, new_second


def solution(mesh):
    in_specs = (
        P(("dp", "tensor"), None),
        P("dp", "tensor"),
        P(),
        P("dp", "tensor"),
        P("dp", "tensor"),
        P(),
    )
    out_specs = (P("dp", "tensor"), P("dp", "tensor"), P("dp", "tensor"))
    return jax.shard_map(
        per_device, mesh=mesh, in_specs=in_specs, out_specs=out_specs, check_vma=False
    )
```

```python
import functools

import jax
import jax.numpy as jnp
from jax import lax
from jax.experimental import pallas as pl
from jax.experimental.pallas import tpu as pltpu
from jax.sharding import PartitionSpec as P

MESH = pl.DeviceIdType.MESH
BF, F32 = jnp.bfloat16, jnp.float32
D, F, R = 4096, 11008, 512
TOK = 512
HALF = TOK // 2
NX, NY, NDP = 4, 4, 8
NT = NX * NY
FC = F // NT
DR = D // NDP
PER = R // NDP
CHUNKS = (128, 128, 128, 128)
SHARES = tuple(c // NDP for c in CHUNKS)
STARTS = tuple(sum(SHARES[:i]) for i in range(len(CHUNKS)))
NC = len(CHUNKS)
PIECES = tuple((c, 0, FC) for c in range(NC - 1)) + ((NC - 1, 0, 384), (NC - 1, 384, FC - 384))
NP = len(PIECES)
PIECES_OF = tuple(tuple(p for p in range(NP) if PIECES[p][0] == c) for c in range(NC))
PART_TYPES = tuple(BF for c, _, _ in PIECES)
KSTEPS = 4
KW = D // KSTEPS
GROUP = 4 * HALF
VMEM_MIB = 52
OFFSETS = (0, -1, 1, 2)
FAR_FIRST = (4, 3, 5, 2, 6, 1, 7)


def dot(a, b, ca, cb):
    return lax.dot_general(a, b, (((ca,), (cb,)), ((), ())), preferred_element_type=F32)


def identity():
    rows = lax.broadcasted_iota(jnp.int32, (R, R), 0)
    cols = lax.broadcasted_iota(jnp.int32, (R, R), 1)
    return jnp.where(rows == cols, 1.0, 0.0).astype(BF)


def kernel(
    act_hbm, cot_hbm, proj_hbm, step_hbm, state,
    upd_out, nfirst, nsecond,
    step_now, act, proj, cot, eye, projt, upd_acc,
    *rest,
):
    gath, acc = rest[:NC], rest[NC : 2 * NC]
    rest = rest[2 * NC :]
    part, parts_in, steps = rest[:NP], rest[NP : 2 * NP], rest[2 * NP : 3 * NP]
    load_sem, cot_sem, ssem, rsem, part_ssem, part_rsem, step_ssem, step_rsem = rest[3 * NP :]

    d = lax.axis_index("dp")
    t = lax.axis_index("tensor")
    y, x = t // NX, t % NX
    pos = ((x, y), (y, x))

    def dev(axis, off):
        if axis == 0:
            return {"dp": d, "tensor": y * NX + (x + off + NX) % NX}
        return {"dp": d, "tensor": ((y + off + NY) % NY) * NX + x}

    def peer(j):
        return {"dp": (d + j) % NDP, "tensor": t}

    loads = []
    for k in range(KSTEPS):
        part_k = (pl.ds(0, HALF), pl.ds(k * KW, KW))
        loads.append(pltpu.make_async_copy(act_hbm.at[part_k], act.at[part_k], load_sem.at[2 * k]))
        loads.append(pltpu.make_async_copy(proj_hbm.at[pl.ds(k * KW, KW)], proj.at[pl.ds(k * KW, KW)], load_sem.at[2 * k + 1]))
    late = pl.ds(HALF, HALF)
    late_load = pltpu.make_async_copy(act_hbm.at[late], act.at[late], load_sem.at[2 * KSTEPS + 3])
    loads.append(pltpu.make_async_copy(step_hbm, step_now, load_sem.at[2 * KSTEPS + 2]))
    for c in loads[: 2 * KSTEPS]:
        c.start()
    late_load.start()

    barrier = pltpu.get_barrier_semaphore()
    for axis in (0, 1):
        for off in (1, -1):
            pl.semaphore_signal(barrier, inc=1, device_id=dev(axis, off), device_id_type=MESH)
    for j in range(1, NDP):
        pl.semaphore_signal(barrier, inc=1, device_id=peer(j), device_id_type=MESH)

    cot_loads = {}
    for h in (0, 1):
        for v in range(4):
            for u in range(4):
                tt = v * NX + u if h == 0 else u * NX + v
                cot_loads[h, v, u] = pltpu.make_async_copy(
                    cot_hbm.at[:, pl.ds(tt * TOK + h * HALF, HALF)],
                    cot.at[h, v * 4 + u],
                    cot_sem.at[0],
                )
    eye[...] = identity()

    def place(h, u, v):
        first_pos, second_pos = pos[h]
        return ((second_pos + v + 4) % 4) * 4 + (first_pos + u + 4) % 4

    def send(c, h, i, order, off, u, v, q):
        ref = gath[c].at[h, place(h, u, v)]
        if q is not None:
            ref = ref.at[pl.ds(q * (CHUNKS[c] // 2), CHUNKS[c] // 2)]
        pltpu.make_async_remote_copy(
            ref, ref, ssem.at[c, h], rsem.at[c, h, i],
            device_id=dev(order ^ h, off), device_id_type=MESH,
        ).start()

    def arrived(c, h, i, blocks):
        ref = gath[c].at[h, pl.ds(0, blocks)]
        pltpu.make_async_copy(ref, ref, rsem.at[c, h, i]).wait()

    def own_first(c, h):
        send(c, h, 0, 0, 1, 0, 0, None)
        send(c, h, 0, 0, -1, 0, 0, None)

    def to_second(c, h, k):
        send(c, h, 2 + k, 1, 1, OFFSETS[k], 0, None)
        send(c, h, 2 + k, 1, -1, OFFSETS[k], 0, None)

    def pass_first(c):
        for h in (0, 1):
            arrived(c, h, 0, 2)
            send(c, h, 1, 0, 1, -1, 0, 0)
            send(c, h, 1, 0, -1, 1, 0, 1)

    def far_first(c):
        for h in (0, 1):
            arrived(c, h, 1, 1)

    def pass_second(c, h, k):
        arrived(c, h, 2 + k, 2)
        send(c, h, 6, 1, 1, OFFSETS[k], -1, 0)
        send(c, h, 6, 1, -1, OFFSETS[k], 1, 1)

    def far_second(c, h):
        arrived(c, h, 6, 4)

    def sent(c):
        for h in (0, 1):
            ref = gath[c].at[h, pl.ds(0, 15)]
            pltpu.make_async_copy(ref, ref, ssem.at[c, h]).wait()

    def add_group(c, h, v, fresh=False):
        at = ((pos[h][1] + v + 4) % 4) * 4
        p = jnp.concatenate([gath[c][h, at + u] for u in range(4)], axis=1)
        g = jnp.concatenate([cot[h, at + u] for u in range(4)], axis=1)
        value = dot(p, g, 1, 1)
        if fresh:
            acc[c][...] = value
        else:
            acc[c][...] += value

    def part_copy(p, j):
        return pltpu.make_async_remote_copy(
            part[p].at[(d + j) % NDP], parts_in[p].at[j - 1], part_ssem.at[p], part_rsem.at[p],
            device_id=peer(j), device_id_type=MESH,
        )

    def step_copy(p, j):
        return pltpu.make_async_remote_copy(
            steps[p].at[d], steps[p].at[d], step_ssem.at[p], step_rsem.at[p],
            device_id=peer(j), device_id_type=MESH,
        )

    def seven(ref, sem):
        ref = ref.at[pl.ds(0, NDP - 1)]
        pltpu.make_async_copy(ref, ref, sem).wait()

    def share_parts(p):
        c, start, width = PIECES[p]
        own = acc[c][:, start : start + width]
        part[p][...] = own.reshape(NDP, SHARES[c], width).astype(PART_TYPES[p])
        for j in FAR_FIRST:
            part_copy(p, j).start()

    def adam(p):
        c, start, width = PIECES[p]
        share = SHARES[c]
        cols = slice(start, start + width)
        t_value = step_now[...].astype(F32)
        fix_first = (1.0 / (1.0 - jnp.power(jnp.full((8, 128), 0.9, F32), t_value)))[0:1, 0:1]
        fix_second = (1.0 / (1.0 - jnp.power(jnp.full((8, 128), 0.999, F32), t_value)))[0:1, 0:1]
        grad = acc[c][pl.ds(pl.multiple_of(d * share, share), share), cols]
        seven(parts_in[p], part_rsem.at[p])
        for j in range(1, NDP):
            grad = grad + parts_in[p][j - 1].astype(F32)
        rows = slice(STARTS[c], STARTS[c] + share)
        new_first = 0.9 * state[rows, cols] + 0.1 * grad
        new_second = 0.999 * state[PER + STARTS[c] : PER + STARTS[c] + share, cols] + 0.001 * grad * grad
        nfirst[rows, cols] = new_first
        nsecond[rows, cols] = new_second
        normalized = (new_first * fix_first) / (jnp.sqrt(new_second * fix_second) + 1e-08)
        steps[p][d] = normalized.astype(BF)
        for j in FAR_FIRST:
            step_copy(p, j).start()

    def update(p):
        c, start, width = PIECES[p]
        seven(steps[p], step_rsem.at[p])
        chunk = steps[p][...].astype(F32).reshape(CHUNKS[c], width)
        value = dot(chunk.T.astype(BF), projt[pl.ds(sum(CHUNKS[:c]), CHUNKS[c]), :], 1, 0)
        if c == 0:
            upd_acc[...] = value
        elif c < NC - 1:
            upd_acc[...] += value
        else:
            rows = slice(start, start + width)
            upd_out[rows, :] = (upd_acc[rows, :] + value).astype(BF)

    for h in (0, 1):
        total = None
        if h == 1:
            late_load.wait()
        for k in range(KSTEPS):
            if h == 0:
                loads[2 * k].wait()
                loads[2 * k + 1].wait()
            value = dot(act[pl.ds(h * HALF, HALF), pl.ds(k * KW, KW)], proj[pl.ds(k * KW, KW), :], 1, 0)
            total = value if total is None else total + value
        turned = dot(eye[...], total.astype(BF), 1, 1)
        for c in range(NC):
            rows = [turned[PER * e + STARTS[c] : PER * e + STARTS[c] + SHARES[c]] for e in range(NDP)]
            gath[c][h, place(h, 0, 0)] = jnp.concatenate(rows, axis=0).astype(BF)
        if h == 0:
            pl.semaphore_wait(barrier, 4 + NDP - 1)
            for c in loads[2 * KSTEPS :]:
                c.start()
            for c in cot_loads.values():
                c.start()
        own_first(0, h)
        to_second(0, h, 0)
        for c in range(1, NC):
            own_first(c, h)
    turned = dot(eye[...], proj[pl.ds(pl.multiple_of(d * DR, DR), DR), :], 1, 1)
    for c in range(NC):
        rows = [turned[PER * e + STARTS[c] : PER * e + STARTS[c] + SHARES[c]] for e in range(NDP)]
        projt[pl.ds(sum(CHUNKS[:c]), CHUNKS[c]), :] = jnp.concatenate(rows, axis=0).astype(BF)

    pass_first(0)
    for k in (1, 2):
        for h in (0, 1):
            to_second(0, h, k)
    for c in range(1, NC):
        pass_first(c)
    far_first(0)
    for h in (0, 1):
        to_second(0, h, 3)
    for c in range(1, NC):
        far_first(c)
    for c in loads[2 * KSTEPS :]:
        c.wait()
    pltpu.make_async_copy(cot, cot, cot_sem.at[0]).wait()

    for i in range(NC):
        if i + 1 < NC:
            for k in range(4):
                for h in (0, 1):
                    to_second(i + 1, h, k)
        for k in range(4):
            for h in (0, 1):
                pass_second(i, h, k)
            if k == 0:
                add_group(i, 0, 0, fresh=True)
            if k == 1:
                add_group(i, 1, 0)
                if i >= 2:
                    adam(i - 2)
            if k == 2 and i >= 3:
                update(i - 3)
        add_group(i, 0, -1)
        add_group(i, 0, 1)
        if i >= 1:
            for h in (0, 1):
                far_second(i - 1, h)
                add_group(i - 1, h, 2)
            share_parts(i - 1)
        add_group(i, 1, -1)
        add_group(i, 1, 1)
    for h in (0, 1):
        far_second(NC - 1, h)
        add_group(NC - 1, h, 2)
    for p in PIECES_OF[NC - 1]:
        share_parts(p)
    adam(NC - 2)
    update(NC - 3)
    for c in range(NC):
        sent(c)
    for p in range(NC - 1):
        seven(parts_in[p], part_ssem.at[p])
    for p in PIECES_OF[NC - 1]:
        adam(p)
    for p in range(NC - 2):
        seven(steps[p], step_ssem.at[p])
    update(NC - 2)
    for p in PIECES_OF[NC - 1]:
        update(p)
    for p in PIECES_OF[NC - 1]:
        seven(parts_in[p], part_ssem.at[p])
    for p in range(NC - 2, NP):
        seven(steps[p], step_ssem.at[p])


def write_out(*arrays):
    def body(*refs):
        n = len(arrays)
        copies = [
            pltpu.make_async_copy(refs[i], refs[n + i], refs[2 * n].at[i]) for i in range(n)
        ]
        for c in copies:
            c.start()
        for c in copies:
            c.wait()

    return pl.pallas_call(
        body,
        out_shape=tuple(jax.ShapeDtypeStruct(a.shape, a.dtype) for a in arrays),
        in_specs=[pl.BlockSpec(memory_space=pltpu.VMEM)] * len(arrays),
        out_specs=[pl.BlockSpec(memory_space=pltpu.HBM)] * len(arrays),
        scratch_shapes=[pltpu.SemaphoreType.DMA((len(arrays),))],
        compiler_params=pltpu.CompilerParams(vmem_limit_bytes=2 * 2**20),
    )(*arrays)


def per_device(activations, cotangent, projection, first_moment, second_moment, step_count):
    scratch = [
        pltpu.VMEM((8, 128), jnp.int32),
        pltpu.VMEM((TOK, D), BF),
        pltpu.VMEM((D, R), BF),
        pltpu.VMEM((2, NT, FC, HALF), BF),
        pltpu.VMEM((R, R), BF),
        pltpu.VMEM((R, DR), BF),
        pltpu.VMEM((FC, DR), F32),
    ]
    scratch += [pltpu.VMEM((2, NT, c, HALF), BF) for c in CHUNKS]
    scratch += [pltpu.VMEM((c, FC), F32) for c in CHUNKS]
    scratch += [pltpu.VMEM((NDP, SHARES[c], w), ty) for (c, _, w), ty in zip(PIECES, PART_TYPES)]
    scratch += [pltpu.VMEM((NDP - 1, SHARES[c], w), ty) for (c, _, w), ty in zip(PIECES, PART_TYPES)]
    scratch += [pltpu.VMEM((NDP, SHARES[c], w), BF) for c, _, w in PIECES]
    dma = pltpu.SemaphoreType.DMA
    scratch += [
        dma((2 * KSTEPS + 4,)), dma((1,)), dma((NC, 2)), dma((NC, 2, 7)),
        dma((NP,)), dma((NP,)), dma((NP,)), dma((NP,)),
    ]
    update_t, new_first, new_second = pl.pallas_call(
        kernel,
        out_shape=(
            jax.ShapeDtypeStruct((FC, DR), BF),
            jax.ShapeDtypeStruct((PER, FC), F32),
            jax.ShapeDtypeStruct((PER, FC), F32),
        ),
        in_specs=[pl.BlockSpec(memory_space=pltpu.HBM)] * 4 + [pl.BlockSpec(memory_space=pltpu.VMEM)],
        out_specs=[pl.BlockSpec(memory_space=pltpu.VMEM)] * 3,
        scratch_shapes=scratch,
        compiler_params=pltpu.CompilerParams(
            collective_id=0, has_side_effects=True, vmem_limit_bytes=int(VMEM_MIB * 2**20)
        ),
        cost_estimate=pl.CostEstimate(flops=9 * 10**9, bytes_accessed=25 * 10**6, transcendentals=0),
    )(activations, cotangent.T, projection, jnp.pad(step_count.reshape(1, 1), ((0, 7), (0, 127))), jnp.concatenate([first_moment, second_moment], axis=0))
    update_t, new_first, new_second = write_out(update_t, new_first, new_second)
    return update_t.T, new_first, new_second


def solution(mesh):
    in_specs = (
        P(("dp", "tensor"), None),
        P("dp", "tensor"),
        P(),
        P("dp", "tensor"),
        P("dp", "tensor"),
        P(),
    )
    out_specs = (P("dp", "tensor"), P("dp", "tensor"), P("dp", "tensor"))
    return jax.shard_map(
        per_device, mesh=mesh, in_specs=in_specs, out_specs=out_specs, check_vma=False
    )
```

```python
import functools

import jax
import jax.numpy as jnp
from jax import lax
from jax.experimental import pallas as pl
from jax.experimental.pallas import tpu as pltpu
from jax.sharding import PartitionSpec as P

MESH = pl.DeviceIdType.MESH
BF, F32 = jnp.bfloat16, jnp.float32
D, F, R = 4096, 11008, 512
TOK = 512
HALF = TOK // 2
NX, NY, NDP = 4, 4, 8
NT = NX * NY
FC = F // NT
DR = D // NDP
PER = R // NDP
CHUNKS = (128, 128, 128, 128)
SHARES = tuple(c // NDP for c in CHUNKS)
STARTS = tuple(sum(SHARES[:i]) for i in range(len(CHUNKS)))
NC = len(CHUNKS)
PIECES = tuple((c, 0, FC) for c in range(NC - 1)) + ((NC - 1, 0, 256), (NC - 1, 256, FC - 256))
NP = len(PIECES)
PIECES_OF = tuple(tuple(p for p in range(NP) if PIECES[p][0] == c) for c in range(NC))
PART_TYPES = tuple(BF for c, _, _ in PIECES)
KSTEPS = 4
KW = D // KSTEPS
GROUP = 4 * HALF
VMEM_MIB = 52
OFFSETS = (0, -1, 1, 2)
FAR_FIRST = (4, 3, 5, 2, 6, 1, 7)


def dot(a, b, ca, cb):
    return lax.dot_general(a, b, (((ca,), (cb,)), ((), ())), preferred_element_type=F32)


def identity():
    rows = lax.broadcasted_iota(jnp.int32, (R, R), 0)
    cols = lax.broadcasted_iota(jnp.int32, (R, R), 1)
    return jnp.where(rows == cols, 1.0, 0.0).astype(BF)


def kernel(
    act_hbm, cot_hbm, proj_hbm, step_hbm, state,
    upd_out, nfirst, nsecond,
    step_now, act, proj, cot, eye, projt, upd_acc,
    *rest,
):
    gath, acc = rest[:NC], rest[NC : 2 * NC]
    rest = rest[2 * NC :]
    part, parts_in, steps = rest[:NP], rest[NP : 2 * NP], rest[2 * NP : 3 * NP]
    load_sem, cot_sem, ssem, rsem, part_ssem, part_rsem, step_ssem, step_rsem = rest[3 * NP :]

    d = lax.axis_index("dp")
    t = lax.axis_index("tensor")
    y, x = t // NX, t % NX
    pos = ((x, y), (y, x))

    def dev(axis, off):
        if axis == 0:
            return {"dp": d, "tensor": y * NX + (x + off + NX) % NX}
        return {"dp": d, "tensor": ((y + off + NY) % NY) * NX + x}

    def peer(j):
        return {"dp": (d + j) % NDP, "tensor": t}

    loads = []
    for k in range(KSTEPS):
        part_k = (pl.ds(0, HALF), pl.ds(k * KW, KW))
        loads.append(pltpu.make_async_copy(act_hbm.at[part_k], act.at[part_k], load_sem.at[2 * k]))
        loads.append(pltpu.make_async_copy(proj_hbm.at[pl.ds(k * KW, KW)], proj.at[pl.ds(k * KW, KW)], load_sem.at[2 * k + 1]))
    late = pl.ds(HALF, HALF)
    late_load = pltpu.make_async_copy(act_hbm.at[late], act.at[late], load_sem.at[2 * KSTEPS + 3])
    loads.append(pltpu.make_async_copy(step_hbm, step_now, load_sem.at[2 * KSTEPS + 2]))
    for c in loads[: 2 * KSTEPS]:
        c.start()
    late_load.start()

    barrier = pltpu.get_barrier_semaphore()
    for axis in (0, 1):
        for off in (1, -1):
            pl.semaphore_signal(barrier, inc=1, device_id=dev(axis, off), device_id_type=MESH)
    for j in range(1, NDP):
        pl.semaphore_signal(barrier, inc=1, device_id=peer(j), device_id_type=MESH)

    cot_loads = {}
    for h in (0, 1):
        for v in range(4):
            for u in range(4):
                tt = v * NX + u if h == 0 else u * NX + v
                cot_loads[h, v, u] = pltpu.make_async_copy(
                    cot_hbm.at[:, pl.ds(tt * TOK + h * HALF, HALF)],
                    cot.at[h, v * 4 + u],
                    cot_sem.at[0],
                )
    eye[...] = identity()

    def place(h, u, v):
        first_pos, second_pos = pos[h]
        return ((second_pos + v + 4) % 4) * 4 + (first_pos + u + 4) % 4

    def send(c, h, i, order, off, u, v, q):
        ref = gath[c].at[h, place(h, u, v)]
        if q is not None:
            ref = ref.at[pl.ds(q * (CHUNKS[c] // 2), CHUNKS[c] // 2)]
        pltpu.make_async_remote_copy(
            ref, ref, ssem.at[c, h], rsem.at[c, h, i],
            device_id=dev(order ^ h, off), device_id_type=MESH,
        ).start()

    def arrived(c, h, i, blocks):
        ref = gath[c].at[h, pl.ds(0, blocks)]
        pltpu.make_async_copy(ref, ref, rsem.at[c, h, i]).wait()

    def own_first(c, h):
        send(c, h, 0, 0, 1, 0, 0, None)
        send(c, h, 0, 0, -1, 0, 0, None)

    def to_second(c, h, k):
        send(c, h, 2 + k, 1, 1, OFFSETS[k], 0, None)
        send(c, h, 2 + k, 1, -1, OFFSETS[k], 0, None)

    def pass_first(c):
        for h in (0, 1):
            arrived(c, h, 0, 2)
            send(c, h, 1, 0, 1, -1, 0, 0)
            send(c, h, 1, 0, -1, 1, 0, 1)

    def far_first(c):
        for h in (0, 1):
            arrived(c, h, 1, 1)

    def pass_second(c, h, k):
        arrived(c, h, 2 + k, 2)
        send(c, h, 6, 1, 1, OFFSETS[k], -1, 0)
        send(c, h, 6, 1, -1, OFFSETS[k], 1, 1)

    def far_second(c, h):
        arrived(c, h, 6, 4)

    def sent(c):
        for h in (0, 1):
            ref = gath[c].at[h, pl.ds(0, 15)]
            pltpu.make_async_copy(ref, ref, ssem.at[c, h]).wait()

    def add_group(c, h, v, fresh=False, cols=slice(0, FC)):
        at = ((pos[h][1] + v + 4) % 4) * 4
        p = jnp.concatenate([gath[c][h, at + u] for u in range(4)], axis=1)
        g = jnp.concatenate([cot[h, at + u, cols, :] for u in range(4)], axis=1)
        value = dot(p, g, 1, 1)
        if fresh:
            acc[c][...] = value
        else:
            acc[c][:, cols] += value

    def part_copy(p, j):
        return pltpu.make_async_remote_copy(
            part[p].at[(d + j) % NDP], parts_in[p].at[j - 1], part_ssem.at[p], part_rsem.at[p],
            device_id=peer(j), device_id_type=MESH,
        )

    def step_copy(p, j):
        return pltpu.make_async_remote_copy(
            steps[p].at[d], steps[p].at[d], step_ssem.at[p], step_rsem.at[p],
            device_id=peer(j), device_id_type=MESH,
        )

    def seven(ref, sem):
        ref = ref.at[pl.ds(0, NDP - 1)]
        pltpu.make_async_copy(ref, ref, sem).wait()

    def share_parts(p):
        c, start, width = PIECES[p]
        own = acc[c][:, start : start + width]
        part[p][...] = own.reshape(NDP, SHARES[c], width).astype(PART_TYPES[p])
        for j in FAR_FIRST:
            part_copy(p, j).start()

    def adam(p):
        c, start, width = PIECES[p]
        share = SHARES[c]
        cols = slice(start, start + width)
        t_value = step_now[...].astype(F32)
        fix_first = (1.0 / (1.0 - jnp.power(jnp.full((8, 128), 0.9, F32), t_value)))[0:1, 0:1]
        fix_second = (1.0 / (1.0 - jnp.power(jnp.full((8, 128), 0.999, F32), t_value)))[0:1, 0:1]
        grad = acc[c][pl.ds(pl.multiple_of(d * share, share), share), cols]
        seven(parts_in[p], part_rsem.at[p])
        for j in range(1, NDP):
            grad = grad + parts_in[p][j - 1].astype(F32)
        rows = slice(STARTS[c], STARTS[c] + share)
        new_first = 0.9 * state[rows, cols] + 0.1 * grad
        new_second = 0.999 * state[PER + STARTS[c] : PER + STARTS[c] + share, cols] + 0.001 * grad * grad
        nfirst[rows, cols] = new_first
        nsecond[rows, cols] = new_second
        normalized = (new_first * fix_first) / (jnp.sqrt(new_second * fix_second) + 1e-08)
        steps[p][d] = normalized.astype(BF)
        for j in FAR_FIRST:
            step_copy(p, j).start()

    def update(p):
        c, start, width = PIECES[p]
        seven(steps[p], step_rsem.at[p])
        chunk = steps[p][...].astype(F32).reshape(CHUNKS[c], width)
        value = dot(chunk.T.astype(BF), projt[pl.ds(sum(CHUNKS[:c]), CHUNKS[c]), :], 1, 0)
        if c == 0:
            upd_acc[...] = value
        elif c < NC - 1:
            upd_acc[...] += value
        else:
            rows = slice(start, start + width)
            upd_out[rows, :] = (upd_acc[rows, :] + value).astype(BF)

    for h in (0, 1):
        total = None
        if h == 1:
            late_load.wait()
        for k in range(KSTEPS):
            if h == 0:
                loads[2 * k].wait()
                loads[2 * k + 1].wait()
            value = dot(act[pl.ds(h * HALF, HALF), pl.ds(k * KW, KW)], proj[pl.ds(k * KW, KW), :], 1, 0)
            total = value if total is None else total + value
        turned = dot(eye[...], total.astype(BF), 1, 1)
        for c in range(NC):
            rows = [turned[PER * e + STARTS[c] : PER * e + STARTS[c] + SHARES[c]] for e in range(NDP)]
            gath[c][h, place(h, 0, 0)] = jnp.concatenate(rows, axis=0).astype(BF)
        if h == 0:
            pl.semaphore_wait(barrier, 4 + NDP - 1)
        own_first(0, h)
        to_second(0, h, 0)
        for c in range(1, NC):
            own_first(c, h)
        if h == 0:
            for c in loads[2 * KSTEPS :]:
                c.start()
            for c in cot_loads.values():
                c.start()
    turned = dot(eye[...], proj[pl.ds(pl.multiple_of(d * DR, DR), DR), :], 1, 1)
    for c in range(NC):
        rows = [turned[PER * e + STARTS[c] : PER * e + STARTS[c] + SHARES[c]] for e in range(NDP)]
        projt[pl.ds(sum(CHUNKS[:c]), CHUNKS[c]), :] = jnp.concatenate(rows, axis=0).astype(BF)

    pass_first(0)
    for k in (1, 2):
        for h in (0, 1):
            to_second(0, h, k)
    for c in range(1, NC):
        pass_first(c)
    far_first(0)
    for h in (0, 1):
        to_second(0, h, 3)
    for c in range(1, NC):
        far_first(c)
    for c in loads[2 * KSTEPS :]:
        c.wait()
    pltpu.make_async_copy(cot, cot, cot_sem.at[0]).wait()

    for i in range(NC):
        if i + 1 < NC:
            for k in range(4):
                for h in (0, 1):
                    to_second(i + 1, h, k)
        for k in range(4):
            for h in (0, 1):
                pass_second(i, h, k)
            if k == 0:
                add_group(i, 0, 0, fresh=True)
            if k == 1:
                add_group(i, 1, 0)
                if i >= 2:
                    adam(i - 2)
            if k == 2 and i >= 3:
                update(i - 3)
        add_group(i, 0, -1)
        add_group(i, 0, 1)
        if i >= 1:
            for h in (0, 1):
                far_second(i - 1, h)
                add_group(i - 1, h, 2)
            share_parts(i - 1)
        add_group(i, 1, -1)
        add_group(i, 1, 1)
    far_second(NC - 1, 0)
    add_group(NC - 1, 0, 2)
    far_second(NC - 1, 1)
    for p in PIECES_OF[NC - 1]:
        add_group(NC - 1, 1, 2, cols=slice(PIECES[p][1], PIECES[p][1] + PIECES[p][2]))
        share_parts(p)
    adam(NC - 2)
    update(NC - 3)
    for c in range(NC):
        sent(c)
    for p in range(NC - 1):
        seven(parts_in[p], part_ssem.at[p])
    for p in PIECES_OF[NC - 1]:
        adam(p)
    for p in range(NC - 2):
        seven(steps[p], step_ssem.at[p])
    update(NC - 2)
    for p in PIECES_OF[NC - 1]:
        update(p)
    for p in PIECES_OF[NC - 1]:
        seven(parts_in[p], part_ssem.at[p])
    for p in range(NC - 2, NP):
        seven(steps[p], step_ssem.at[p])


def write_out(*arrays):
    def body(*refs):
        n = len(arrays)
        copies = [
            pltpu.make_async_copy(refs[i], refs[n + i], refs[2 * n].at[i]) for i in range(n)
        ]
        for c in copies:
            c.start()
        for c in copies:
            c.wait()

    return pl.pallas_call(
        body,
        out_shape=tuple(jax.ShapeDtypeStruct(a.shape, a.dtype) for a in arrays),
        in_specs=[pl.BlockSpec(memory_space=pltpu.VMEM)] * len(arrays),
        out_specs=[pl.BlockSpec(memory_space=pltpu.HBM)] * len(arrays),
        scratch_shapes=[pltpu.SemaphoreType.DMA((len(arrays),))],
        compiler_params=pltpu.CompilerParams(vmem_limit_bytes=2 * 2**20),
    )(*arrays)


def per_device(activations, cotangent, projection, first_moment, second_moment, step_count):
    scratch = [
        pltpu.VMEM((8, 128), jnp.int32),
        pltpu.VMEM((TOK, D), BF),
        pltpu.VMEM((D, R), BF),
        pltpu.VMEM((2, NT, FC, HALF), BF),
        pltpu.VMEM((R, R), BF),
        pltpu.VMEM((R, DR), BF),
        pltpu.VMEM((FC, DR), F32),
    ]
    scratch += [pltpu.VMEM((2, NT, c, HALF), BF) for c in CHUNKS]
    scratch += [pltpu.VMEM((c, FC), F32) for c in CHUNKS]
    scratch += [pltpu.VMEM((NDP, SHARES[c], w), ty) for (c, _, w), ty in zip(PIECES, PART_TYPES)]
    scratch += [pltpu.VMEM((NDP - 1, SHARES[c], w), ty) for (c, _, w), ty in zip(PIECES, PART_TYPES)]
    scratch += [pltpu.VMEM((NDP, SHARES[c], w), BF) for c, _, w in PIECES]
    dma = pltpu.SemaphoreType.DMA
    scratch += [
        dma((2 * KSTEPS + 4,)), dma((1,)), dma((NC, 2)), dma((NC, 2, 7)),
        dma((NP,)), dma((NP,)), dma((NP,)), dma((NP,)),
    ]
    update_t, new_first, new_second = pl.pallas_call(
        kernel,
        out_shape=(
            jax.ShapeDtypeStruct((FC, DR), BF),
            jax.ShapeDtypeStruct((PER, FC), F32),
            jax.ShapeDtypeStruct((PER, FC), F32),
        ),
        in_specs=[pl.BlockSpec(memory_space=pltpu.HBM)] * 4 + [pl.BlockSpec(memory_space=pltpu.VMEM)],
        out_specs=[pl.BlockSpec(memory_space=pltpu.VMEM)] * 3,
        scratch_shapes=scratch,
        compiler_params=pltpu.CompilerParams(
            collective_id=0, has_side_effects=True, vmem_limit_bytes=int(VMEM_MIB * 2**20)
        ),
        cost_estimate=pl.CostEstimate(flops=9 * 10**9, bytes_accessed=25 * 10**6, transcendentals=0),
    )(activations, cotangent.T, projection, jnp.pad(step_count.reshape(1, 1), ((0, 7), (0, 127))), jnp.concatenate([first_moment, second_moment], axis=0))
    update_t, new_first, new_second = write_out(update_t, new_first, new_second)
    return update_t.T, new_first, new_second


def solution(mesh):
    in_specs = (
        P(("dp", "tensor"), None),
        P("dp", "tensor"),
        P(),
        P("dp", "tensor"),
        P("dp", "tensor"),
        P(),
    )
    out_specs = (P("dp", "tensor"), P("dp", "tensor"), P("dp", "tensor"))
    return jax.shard_map(
        per_device, mesh=mesh, in_specs=in_specs, out_specs=out_specs, check_vma=False
    )
```
